32 devices in a mesh: layer: 4 (over y, x), node: 8 (over z, core).
Axes of the slice: x: 2, y: 2, z: 4, core: 2. Of those that a mesh axis runs over, the one named last changes fastest.
Arguments:
- features: bfloat16 [4, 2048, 512], P(None, 'node'), may hold values from -6 to 6
- w_self: bfloat16 [4, 512, 512], P('layer'), may hold values from -0.1875 to 0.1875
- w_neigh: bfloat16 [4, 512, 512], P('layer'), may hold values from -0.1875 to 0.1875
- w_out: bfloat16 [512, 172], replicated, may hold values from -0.25 to 0.25
- labels: int32 [4, 2048], P(None, 'node'), may hold values from 0 to 171
- train_mask: int32 [4, 2048], P(None, 'node'), may hold values 0 or 1
- tile_cols: int32 [4, 8, 2, 4], P(None, 'node'), may hold values from 0 to 2
- tile_vals: bfloat16 [4, 8, 2, 4, 128, 128], P(None, 'node'), may hold values from -0.25 to 0.25
- send_rows: int32 [4, 8, 8, 8], P(None, 'node'), may hold values from 0 to 255
- send_counts: int32 [4, 8, 8], P(None, 'node'), may hold values from 0 to 8, as said below
Outputs:
- layer_acts: bfloat16 [4, 4, 2048, 512], P('layer', None, 'node')
- act_grads: bfloat16 [4, 4, 2048, 512], P('layer', None, 'node')
- grad_self: float32 [4, 512, 512], P('layer')
- grad_neigh: float32 [4, 512, 512], P('layer')
The draws below stay inside these ranges and needn't reach their ends.
Inputs may be any that keep to these rules, and one draw needn't show every extreme that they name: `send_counts`: in every span one partition, drawn per span, gets 8 rows from every partition, itself included; the other counts are at most 4. `send_rows`: entries of slots at or past the count are ignored; rows may repeat. `tile_cols`: A value below 2 is a tile of the partition's own rows; larger values are tiles of the received rows in source order, 8 slots per source, then zero rows; tiles of a row tile may repeat.
All inputs are finite; a program needn't handle non-finite values. No bound on the sum of `train_mask` on one device may be relied on, other than what follows from the above.
Results may differ from the reference program's by a relative error of at most 0.03.
Values may be sent and summed in bfloat16 or wider, within the bound.
A program may use at most 128 MiB of HBM per device.

```python
import jax
import jax.numpy as jnp

D = 512
C = 172
NR = 256
M = 4
TILE = 128
DEG = 4
CAP = 8
NODES = 2048
WIN_NODES = 8192
N_LAYER = 4
N_NODE = 8


def draw_send_counts(key, part):
    key_counts, key_target = jax.random.split(jax.random.fold_in(key, 17))
    base_counts = jax.random.randint(key_counts, (M, N_NODE, N_NODE), CAP // 8, CAP // 2 + 1)
    busy_target = jax.random.randint(key_target, (M,), 0, N_NODE)
    is_busy = jnp.arange(N_NODE)[None, None, :] == busy_target[:, None, None]
    return jnp.where(is_busy, CAP, base_counts).astype(jnp.int32)


def set_ends(entries, own_key, low, high):
    index_at = [jax.random.randint(jax.random.fold_in(own_key, axis), (), 0, length) for axis, length in enumerate(entries.shape)]
    longest = entries.shape.index(max(entries.shape))
    neighbour = index_at[:longest] + [(index_at[longest] + 1) % entries.shape[longest]] + index_at[longest + 1:]
    return entries.at[tuple(index_at)].set(low).at[tuple(neighbour)].set(high)


def block_levels(key, shape, cuts, low, top_value):
    def one(axis_at, blocks):
        draws = jax.random.uniform(jax.random.fold_in(jax.random.fold_in(key, 6), axis_at), (blocks,), jnp.float32, low / len(cuts), top_value / len(cuts))
        return jnp.repeat(jnp.exp(draws), shape[axis_at] // blocks).reshape((-1,) + (1,) * (len(shape) - axis_at - 1))

    loudness = one(*cuts[0])
    for cut in cuts[1:]:
        loudness = loudness * one(*cut)
    return loudness


def noise(stream_key, dims, scale, most, cuts=(), kind=jnp.bfloat16):
    array = scale * jax.random.normal(stream_key, dims, jnp.float32)
    if cuts:
        array = array * block_levels(stream_key, dims, cuts, -0.22, 0.18)
    return jnp.clip(array, -most, most).astype(kind)


def setup_inputs(seed: int = 0) -> dict:
    keys = jax.random.split(jax.random.key(seed), 11)
    return {
        "features": noise(keys[0], (M, NODES, D), 1.0, 6.0, ((1, 8),)),
        "w_self": noise(keys[1], (N_LAYER, D, D), (2 * D) ** -0.5, 0.1875, ((0, 4),)),
        "w_neigh": noise(keys[2], (N_LAYER, D, D), (2 * D) ** -0.5, 0.1875, ((0, 4),)),
        "w_out": noise(keys[3], (D, C), D ** -0.5, 0.25),
        "labels": set_ends(jax.random.randint(keys[4], (M, NODES), 0, C), jax.random.fold_in(keys[4], 1), 0, C - 1).astype(jnp.int32),
        "train_mask": set_ends((jax.random.randint(keys[5], (M, NODES), 0, 2) < 1).astype(jnp.int32), jax.random.fold_in(keys[5], 1), 0, 1),
        "tile_cols": set_ends(jax.random.randint(keys[6], (M, N_NODE, NR // TILE, DEG), 0, (NR + N_NODE * CAP + TILE - 1) // TILE), jax.random.fold_in(keys[6], 1), 0, ((NR + N_NODE * CAP + TILE - 1) // TILE) - 1).astype(jnp.int32),
        "tile_vals": noise(keys[7], (M, N_NODE, NR // TILE, DEG, TILE, TILE), (TILE * DEG) ** -0.5, 0.25, ((1, 8),)),
        "send_rows": set_ends(jax.random.randint(keys[8], (M, N_NODE, N_NODE, CAP), 0, NR), jax.random.fold_in(keys[8], 1), 0, NR - 1).astype(jnp.int32),
        "send_counts": draw_send_counts(jax.random.fold_in(keys[10], 71), 0),
    }


def silu_slope(preact):
    sigma = jax.nn.sigmoid(preact)
    return sigma * (1.0 + preact * (1.0 - sigma))


def extend_rows(hidden_in, arrived):
    extended = jnp.concatenate([hidden_in, arrived], axis=0)
    ext_len = extended.shape[0]
    padded_len = (ext_len + TILE - 1) // TILE * TILE
    return jnp.pad(extended, ((0, padded_len - ext_len), (0, 0)))


def aggregate_part(extended, col_tiles, values):
    blocks = jnp.take(extended.reshape(-1, TILE, D), col_tiles, axis=0)
    summed = jnp.einsum("rkij,rkjd->rid", values.astype(jnp.float32), blocks.astype(jnp.float32))
    return summed.reshape(NR, D).astype(jnp.bfloat16)


def spread_part(d_agg, col_tiles, values):
    ext_rows = (NR + N_NODE * CAP + TILE - 1) // TILE * TILE
    pieces = jnp.einsum("rkij,rid->rkjd", values.astype(jnp.float32), d_agg.reshape(-1, TILE, D).astype(jnp.float32))
    d_ext = jax.ops.segment_sum(pieces.reshape(-1, TILE, D), col_tiles.reshape(-1), num_segments=ext_rows // TILE)
    return d_ext.reshape(ext_rows, D)


def take_rows(hidden, rows):
    return jnp.take(hidden, rows, axis=0)


def scatter_rows(masked, rows):
    return jax.ops.segment_sum(masked.reshape(-1, D), rows.reshape(-1), num_segments=NR)


def reference(features, w_self, w_neigh, w_out, labels, train_mask, tile_cols, tile_vals, send_rows, send_counts):
    acts_all = [[None] * M for layer_idx in range(N_LAYER)]
    grads_all = [[None] * M for layer_idx in range(N_LAYER)]
    g_self = [jnp.zeros((D, D), jnp.float32) for layer_idx in range(N_LAYER)]
    g_neigh = [jnp.zeros((D, D), jnp.float32) for layer_idx in range(N_LAYER)]
    for span_idx in range(M):
        col_tiles = tile_cols[span_idx]
        values = tile_vals[span_idx]
        rows = send_rows[span_idx]
        is_live = jnp.arange(CAP)[None, None, :] < send_counts[span_idx][:, :, None]
        hidden = features[span_idx].reshape(N_NODE, NR, D)
        saved = []
        for layer_idx in range(N_LAYER):
            sent = jax.vmap(take_rows)(hidden, rows)
            sent = jnp.where(is_live[..., None], sent, jnp.zeros((), jnp.bfloat16))
            arrived = jnp.swapaxes(sent, 0, 1).reshape(N_NODE, N_NODE * CAP, D)
            extended = jax.vmap(extend_rows)(hidden, arrived)
            aggregate = jax.vmap(aggregate_part)(extended, col_tiles, values)
            preact = jnp.einsum("pnd,de->pne", hidden.astype(jnp.float32), w_self[layer_idx].astype(jnp.float32))
            preact = preact + jnp.einsum("pnd,de->pne", aggregate.astype(jnp.float32), w_neigh[layer_idx].astype(jnp.float32))
            output = jax.nn.silu(preact).astype(jnp.bfloat16)
            saved.append((hidden, aggregate, preact))
            acts_all[layer_idx][span_idx] = output.reshape(NODES, D)
            hidden = output
        logits = jnp.einsum("pnd,dc->pnc", hidden.astype(jnp.float32), w_out.astype(jnp.float32))
        expo = jnp.exp(logits)
        probs = expo / jnp.sum(expo, axis=-1, keepdims=True)
        label_rows = labels[span_idx].reshape(N_NODE, NR)
        onehot = (label_rows[..., None] == jnp.arange(C)[None, None, :]).astype(jnp.float32)
        mask_rows = train_mask[span_idx].reshape(N_NODE, NR, 1).astype(jnp.float32)
        g_logits = (mask_rows * (probs - onehot)).astype(jnp.bfloat16)
        d_out = jnp.einsum("pnc,dc->pnd", g_logits.astype(jnp.float32), w_out.astype(jnp.float32)).astype(jnp.bfloat16)
        for layer_idx in range(N_LAYER - 1, -1, -1):
            hidden_in, aggregate, preact = saved[layer_idx]
            d_pre = (d_out.astype(jnp.float32) * silu_slope(preact)).astype(jnp.bfloat16)
            g_self[layer_idx] = g_self[layer_idx] + jnp.einsum("pnd,pne->de", hidden_in.astype(jnp.float32), d_pre.astype(jnp.float32))
            g_neigh[layer_idx] = g_neigh[layer_idx] + jnp.einsum("pnd,pne->de", aggregate.astype(jnp.float32), d_pre.astype(jnp.float32))
            back_self = jnp.einsum("pne,de->pnd", d_pre.astype(jnp.float32), w_self[layer_idx].astype(jnp.float32))
            d_agg = jnp.einsum("pne,de->pnd", d_pre.astype(jnp.float32), w_neigh[layer_idx].astype(jnp.float32)).astype(jnp.bfloat16)
            d_ext = jax.vmap(spread_part)(d_agg, col_tiles, values)
            local_part = d_ext[:, :NR]
            d_sent = d_ext[:, NR:NR + N_NODE * CAP].reshape(N_NODE, N_NODE, CAP, D).astype(jnp.bfloat16)
            returned = jnp.swapaxes(d_sent, 0, 1)
            masked = jnp.where(is_live[..., None], returned.astype(jnp.float32), jnp.zeros((), jnp.float32))
            scattered = jax.vmap(scatter_rows)(masked, rows)
            d_in = (back_self + local_part + scattered).astype(jnp.bfloat16)
            grads_all[layer_idx][span_idx] = d_in.reshape(NODES, D)
            d_out = d_in
    layer_acts = jnp.stack([jnp.stack(acts_all[layer_idx]) for layer_idx in range(N_LAYER)])
    act_grads = jnp.stack([jnp.stack(grads_all[layer_idx]) for layer_idx in range(N_LAYER)])
    grad_self = jnp.stack(g_self) / WIN_NODES
    grad_neigh = jnp.stack(g_neigh) / WIN_NODES
    return (layer_acts, act_grads, grad_self, grad_neigh)
```

```python
import jax
import jax.numpy as jnp
from jax import lax
from jax.sharding import PartitionSpec as P


def pick(array, index):
    return lax.dynamic_index_in_dim(array, index, 0, keepdims=False)


def dot(a, b, dims=((1,), (0,))):
    return lax.dot_general(a, b, (dims, ((), ())), preferred_element_type=jnp.float32)


def dense_tiles(col_tiles, values, col_count):
    row_tiles, degree, tile, _ = values.shape
    chosen = col_tiles[:, :, None] == jnp.arange(col_count)[None, None, :]
    wide = jnp.where(chosen[:, :, :, None, None], values[:, :, None].astype(jnp.float32), 0.0)
    return jnp.sum(wide, axis=1).transpose(0, 2, 1, 3).reshape(row_tiles * tile, col_count * tile).astype(jnp.bfloat16)


def slot_selector(send_list, counts, node_rows):
    peers, slots = send_list.shape
    live = jnp.arange(slots)[None, :] < counts[:, None]
    hit = send_list[:, :, None] == jnp.arange(node_rows)[None, None, :]
    return (hit & live[:, :, None]).astype(jnp.bfloat16).reshape(peers * slots, node_rows)


def swap_rows(rows, peers):
    parts = rows.reshape(peers, -1, rows.shape[-1])
    return lax.all_to_all(parts, "node", split_axis=0, concat_axis=0, tiled=True).reshape(rows.shape)


def body(features, w_self, w_neigh, w_out, labels, train_mask, tile_cols, tile_vals, send_rows, send_counts):
    me = lax.axis_index("layer")
    layers = lax.axis_size("layer")
    peers = lax.axis_size("node")
    spans, node_rows, feat_dim = features.shape
    classes = w_out.shape[1]
    tile = tile_vals.shape[-1]
    slots = send_rows.shape[-1]
    received = peers * slots
    ext_rows = (node_rows + received + tile - 1) // tile * tile
    scale = 1.0 / (spans * node_rows * peers)
    bf16 = jnp.bfloat16

    adjacency = dense_tiles(pick(tile_cols, me)[0], pick(tile_vals, me)[0], ext_rows // tile)
    adjacency = adjacency[:, : node_rows + received]
    selector = slot_selector(pick(send_rows, me)[0], pick(send_counts, me)[0], node_rows)
    weights_self = lax.all_gather(w_self[0], "layer")
    weights_neigh = lax.all_gather(w_neigh[0], "layer")

    hidden = pick(features, me)
    saved = []
    acts = []
    for layer in range(layers):
        arrived = swap_rows(dot(selector, hidden).astype(bf16), peers)
        aggregate = dot(adjacency, jnp.concatenate([hidden, arrived], axis=0)).astype(bf16)
        preact = dot(hidden, weights_self[layer]) + dot(aggregate, weights_neigh[layer])
        saved.append((hidden, aggregate, preact))
        hidden = jax.nn.silu(preact).astype(bf16)
        acts.append(hidden)

    logits = dot(hidden, w_out)
    expo = jnp.exp(logits)
    probs = expo / jnp.sum(expo, axis=-1, keepdims=True)
    onehot = (pick(labels, me)[:, None] == jnp.arange(classes)[None, :]).astype(jnp.float32)
    g_logits = (pick(train_mask, me)[:, None].astype(jnp.float32) * (probs - onehot)).astype(bf16)
    d_out = dot(g_logits, w_out, ((1,), (1,))).astype(bf16)

    grads = [None] * layers
    weight_grads = [None] * layers
    for layer in range(layers - 1, -1, -1):
        hidden_in, aggregate, preact = saved[layer]
        sigma = jax.nn.sigmoid(preact)
        d_pre = (d_out.astype(jnp.float32) * (sigma * (1.0 + preact * (1.0 - sigma)))).astype(bf16)
        d_agg = dot(d_pre, weights_neigh[layer], ((1,), (1,))).astype(bf16)
        d_ext = dot(adjacency, d_agg, ((0,), (0,)))
        returned = swap_rows(d_ext[node_rows:].astype(bf16), peers)
        weight_grads[layer] = jnp.stack(
            [dot(hidden_in, d_pre, ((0,), (0,))), dot(aggregate, d_pre, ((0,), (0,)))]
        ).astype(bf16)
        back_self = dot(d_pre, weights_self[layer], ((1,), (1,)))
        scattered = dot(selector, returned, ((0,), (0,)))
        d_out = (back_self + d_ext[:node_rows] + scattered).astype(bf16)
        grads[layer] = d_out

    layer_acts = lax.all_to_all(jnp.stack(acts), "layer", split_axis=0, concat_axis=0, tiled=True)
    act_grads = lax.all_to_all(jnp.stack(grads), "layer", split_axis=0, concat_axis=0, tiled=True)
    mine = lax.all_to_all(jnp.stack(weight_grads), "layer", split_axis=0, concat_axis=0, tiled=True)
    mine = jnp.sum(mine.astype(jnp.float32), axis=0).astype(bf16)
    total = lax.psum(mine, "node").astype(jnp.float32) * scale
    return layer_acts[None], act_grads[None], total[0][None], total[1][None]


def solution(mesh):
    in_specs = (
        P(None, "node", None),
        P("layer", None, None),
        P("layer", None, None),
        P(),
        P(None, "node"),
        P(None, "node"),
        P(None, "node", None, None),
        P(None, "node", None, None, None, None),
        P(None, "node", None, None),
        P(None, "node", None),
    )
    out_specs = (
        P("layer", None, "node", None),
        P("layer", None, "node", None),
        P("layer", None, None),
        P("layer", None, None),
    )
    return jax.shard_map(body, mesh=mesh, in_specs=in_specs, out_specs=out_specs, check_vma=False)
```

```python
import functools

import jax
import jax.numpy as jnp
from jax import lax
from jax.experimental import pallas as pl
from jax.experimental.pallas import tpu as pltpu
from jax.sharding import PartitionSpec as P


def pick(array, index):
    return lax.dynamic_index_in_dim(array, index, 0, keepdims=False)


def dot(a, b, dims=((1,), (0,))):
    return lax.dot_general(a, b, (dims, ((), ())), preferred_element_type=jnp.float32)


def dense_tiles(col_tiles, values, col_count):
    row_tiles, degree, tile, _ = values.shape
    chosen = col_tiles[:, :, None] == jnp.arange(col_count)[None, None, :]
    wide = jnp.where(chosen[:, :, :, None, None], values[:, :, None].astype(jnp.float32), 0.0)
    return jnp.sum(wide, axis=1).transpose(0, 2, 1, 3).reshape(row_tiles * tile, col_count * tile).astype(jnp.bfloat16)


def slot_selector(send_list, counts, node_rows):
    peers, slots = send_list.shape
    live = jnp.arange(slots)[None, :] < counts[:, None]
    hit = send_list[:, :, None] == jnp.arange(node_rows)[None, None, :]
    return (hit & live[:, :, None]).astype(jnp.bfloat16).reshape(peers * slots, node_rows)


MESH = pl.DeviceIdType.MESH


def window_kernel(
    layers, peers, slots, classes, scale,
    feats, w_self, w_neigh, w_out, labels, mask, adj, adj_t, sel, sel_t,
    acts_out, grads_out, gself_out, gneigh_out,
    hid, agg, pre, dpre, dout, wts, ext, back, outbox, inbox, rec_hid, rec_agg, rec_dpre,
    gsum, gsend, gsib, chip, parts, final,
    w_send, w_recv, f_send, f_recv, x_send, x_recv, blk_send, blk_recv,
    sib_send, sib_recv, rs_send, rs_recv, ag_send, ag_recv, fw_send, fw_recv,
):
    me = lax.axis_index("layer")
    node = lax.axis_index("node")
    core = lax.rem(node, 2)
    chip_at = node // 2
    chips = peers // 2
    sibling = node + 1 - 2 * core
    node_rows, feat_dim = hid.shape[1:]
    f32, bf16 = jnp.float32, jnp.bfloat16
    chunk = feat_dim // chips

    def remote(src, dst, send, recv, device):
        return pltpu.make_async_remote_copy(
            src_ref=src, dst_ref=dst, send_sem=send, recv_sem=recv, device_id=device, device_id_type=MESH
        )

    def drain(ref, sem):
        pltpu.make_async_copy(ref, ref, sem).wait()

    def each(count, fn, start=0):
        def step(i, carry):
            fn(i)
            return carry
        lax.fori_loop(start, count, step, 0)

    def other_layers(fn):
        each(layers, lambda i: fn(lax.rem(me + i, layers)), 1)

    def other_nodes(fn):
        each(peers, lambda i: fn(lax.rem(node + i, peers)), 1)

    def other_chips(fn):
        each(chips, lambda i: fn(lax.rem(chip_at + i, chips)), 1)

    barrier = pltpu.get_barrier_semaphore()
    other_layers(lambda i: pl.semaphore_signal(barrier, inc=1, device_id=(i, node), device_id_type=MESH))
    other_nodes(lambda i: pl.semaphore_signal(barrier, inc=1, device_id=(me, i), device_id_type=MESH))
    wts[me, 0] = w_self[...]
    wts[me, 1] = w_neigh[...]
    pl.semaphore_wait(barrier, layers - 1 + peers - 1)

    def send_weights(i):
        remote(wts.at[me, core], wts.at[me, core], w_send.at[i], w_recv.at[me], (i, node)).start()

    other_layers(send_weights)

    hid[0] = feats[me]
    ext[...] = jnp.zeros_like(ext)
    back[...] = jnp.zeros_like(back)

    @pl.when(me == 0)
    def _():
        rec_hid[...] = feats[...]

    def swap_start(turn):
        def send(i):
            remote(
                outbox.at[turn, pl.ds(pl.multiple_of(i * slots, slots), slots)],
                inbox.at[turn, pl.ds(pl.multiple_of(node * slots, slots), slots)],
                x_send.at[turn], x_recv.at[turn], (me, i),
            ).start()
        other_nodes(send)
        mine = pl.ds(pl.multiple_of(node * slots, slots), slots)
        inbox[turn, mine] = outbox[turn, mine]

    def swap_bytes(turn):
        return inbox.at[turn, pl.ds(0, (peers - 1) * slots)]

    def give(kind, src, dst, owner):
        @pl.when(owner == me)
        def _():
            dst[me] = src[...]

        @pl.when(owner != me)
        def _():
            remote(src, dst.at[me], blk_send.at[kind, owner], blk_recv.at[kind, me], (owner, node)).start()

    def forward(layer):
        outbox[layer] = dot(sel[...], hid[layer])
        swap_start(layer)

        @pl.when(layer != me)
        def _():
            drain(wts.at[layer, core], w_recv.at[layer])
            remote(wts.at[layer, core], wts.at[layer, core], f_send.at[layer], f_recv.at[layer], (me, sibling)).start()

        ext[:node_rows] = hid[layer]
        drain(swap_bytes(layer), x_recv.at[layer])
        ext[node_rows : node_rows + peers * slots] = inbox[layer, : peers * slots].astype(bf16)
        aggregate = dot(adj[...], ext[...]).astype(bf16)
        agg[layer] = aggregate
        give(0, agg.at[layer], rec_agg, layer)

        @pl.when(layer != me)
        def _():
            drain(wts.at[layer, 1 - core], f_recv.at[layer])

        preact = dot(hid[layer], wts[layer, 0]) + dot(aggregate, wts[layer, 1])
        pre[layer] = preact
        hid[layer + 1] = (preact * jax.nn.sigmoid(preact)).astype(bf16)
        give(1, hid.at[layer + 1], acts_out, layer)

        @pl.when(layer + 1 < layers)
        def _():
            give(2, hid.at[layer + 1], rec_hid, lax.rem(layer + 1, layers))

    each(layers, forward)

    logits = dot(hid[layers], w_out[...])
    real = lax.broadcasted_iota(jnp.int32, logits.shape, 1)
    expo = jnp.where(real < classes, jnp.exp(logits), 0.0)
    probs = expo / jnp.sum(expo, axis=-1, keepdims=True)
    onehot = (labels[...] == real).astype(f32)
    g_logits = (mask[...].astype(f32) * (probs - onehot)).astype(bf16)
    dout[layers] = dot(g_logits, w_out[...], ((1,), (1,))).astype(bf16)

    def backward(turn):
        layer = layers - 1 - turn
        preact = pre[layer]
        sigma = jax.nn.sigmoid(preact)
        d_pre = (dout[layer + 1].astype(f32) * (sigma * (1.0 + preact * (1.0 - sigma)))).astype(bf16)
        dpre[layer] = d_pre
        d_agg = dot(d_pre, wts[layer, 1], ((1,), (1,))).astype(bf16)
        d_ext = dot(adj_t[...], d_agg)
        outbox[layers + turn] = d_ext[node_rows:]
        swap_start(layers + turn)
        give(3, dpre.at[layer], rec_dpre, layer)
        local = dot(d_pre, wts[layer, 0], ((1,), (1,))) + d_ext[:node_rows]
        drain(swap_bytes(layers + turn), x_recv.at[layers + turn])
        back[: peers * slots] = inbox[layers + turn, : peers * slots].astype(bf16)
        dout[layer] = (local + dot(sel_t[...], back[...])).astype(bf16)
        give(4, dout.at[layer], grads_out, layer)

    each(layers, backward)

    gsum[...] = jnp.zeros_like(gsum)

    def add_span(i):
        span = lax.rem(me + i, layers)

        @pl.when(i != 0)
        def _():
            drain(rec_agg.at[span], blk_recv.at[0, span])
            drain(rec_dpre.at[span], blk_recv.at[3, span])

            @pl.when(me != 0)
            def _():
                drain(rec_hid.at[span], blk_recv.at[2, span])

        over_rows = ((0,), (0,))
        gsum[0] += dot(rec_hid[span], rec_dpre[span], over_rows)
        gsum[1] += dot(rec_agg[span], rec_dpre[span], over_rows)

    each(layers, add_span)

    gsend[...] = gsum[1 - core].astype(bf16)
    to_sibling = remote(gsend, gsib, sib_send, sib_recv, (me, sibling))
    to_sibling.start()
    drain(gsib, sib_recv)
    chip[...] = (gsum[core] + gsib[...].astype(f32)).astype(bf16)

    def rows_of(i):
        return pl.ds(pl.multiple_of(i * chunk, chunk), chunk)

    def send_part(i):
        remote(chip.at[rows_of(i)], parts.at[rows_of(chip_at)], rs_send, rs_recv, (me, 2 * i + core)).start()

    other_chips(send_part)
    parts[rows_of(chip_at)] = chip[rows_of(chip_at)]
    drain(parts.at[pl.ds(0, (chips - 1) * chunk)], rs_recv)
    total = parts[pl.ds(0, chunk)].astype(f32)
    for i in range(1, chips):
        total = total + parts[pl.ds(i * chunk, chunk)].astype(f32)
    final[core, rows_of(chip_at)] = total.astype(bf16)

    def send_final(i):
        mine = final.at[core, rows_of(chip_at)]
        remote(mine, mine, ag_send, ag_recv.at[chip_at], (me, 2 * i + core)).start()

    def pass_on(i):
        piece = final.at[core, rows_of(i)]
        remote(piece, piece, fw_send, fw_recv.at[i], (me, sibling)).start()

    other_chips(send_final)
    pass_on(chip_at)

    def take_final(i):
        drain(final.at[core, rows_of(i)], ag_recv.at[i])
        pass_on(i)

    other_chips(take_final)
    each(chips, lambda i: drain(final.at[1 - core, rows_of(i)], fw_recv.at[i]))
    gself_out[...] = final[0].astype(f32) * scale
    gneigh_out[...] = final[1].astype(f32) * scale

    def finish_layer(i):
        drain(acts_out.at[i], blk_recv.at[1, i])
        drain(grads_out.at[i], blk_recv.at[4, i])
        drain(wts.at[me, core], w_send.at[i])
        drain(wts.at[i, core], f_send.at[i])
        drain(agg.at[i], blk_send.at[0, i])
        drain(hid.at[i], blk_send.at[1, i])
        drain(dpre.at[i], blk_send.at[3, i])
        drain(dout.at[i], blk_send.at[4, i])

        @pl.when(i != 0)
        def _():
            drain(hid.at[i], blk_send.at[2, i])

    other_layers(finish_layer)
    each(2 * layers, lambda turn: drain(swap_bytes(turn), x_send.at[turn]))
    drain(gsend, sib_send)
    drain(parts.at[pl.ds(0, (chips - 1) * chunk)], rs_send)
    drain(final.at[0, pl.ds(0, (chips - 1) * chunk)], ag_send)
    drain(final.at[0], fw_send)


def body(features, w_self, w_neigh, w_out, labels, train_mask, tile_cols, tile_vals, send_rows, send_counts):
    me = lax.axis_index("layer")
    layers = lax.axis_size("layer")
    peers = lax.axis_size("node")
    spans, node_rows, feat_dim = features.shape
    classes = w_out.shape[1]
    tile = tile_vals.shape[-1]
    slots = send_rows.shape[-1]
    ext_rows = (node_rows + peers * slots + tile - 1) // tile * tile
    slot_rows = ext_rows - node_rows
    chips = peers // 2
    chunk = feat_dim // chips
    scale = 1.0 / (spans * node_rows * peers)
    f32, bf16 = jnp.float32, jnp.bfloat16

    adjacency = dense_tiles(pick(tile_cols, me)[0], pick(tile_vals, me)[0], ext_rows // tile)
    selector = slot_selector(pick(send_rows, me)[0], pick(send_counts, me)[0], node_rows)
    selector = jnp.pad(selector, ((0, slot_rows - peers * slots), (0, 0)))
    w_out = jnp.pad(w_out, ((0, 0), (0, -classes % 128)))
    block = (layers, node_rows, feat_dim)
    square = (feat_dim, feat_dim)
    vmem = pl.BlockSpec(memory_space=pltpu.VMEM)
    dma = pltpu.SemaphoreType.DMA
    out = pl.pallas_call(
        functools.partial(window_kernel, layers, peers, slots, classes, scale),
        out_shape=(
            jax.ShapeDtypeStruct(block, bf16),
            jax.ShapeDtypeStruct(block, bf16),
            jax.ShapeDtypeStruct(square, f32),
            jax.ShapeDtypeStruct(square, f32),
        ),
        in_specs=[vmem] * 10,
        out_specs=[vmem] * 4,
        scratch_shapes=[
            pltpu.VMEM((layers + 1, node_rows, feat_dim), bf16),
            pltpu.VMEM(block, bf16),
            pltpu.VMEM(block, f32),
            pltpu.VMEM(block, bf16),
            pltpu.VMEM((layers + 1, node_rows, feat_dim), bf16),
            pltpu.VMEM((layers, 2) + square, bf16),
            pltpu.VMEM((ext_rows, feat_dim), bf16),
            pltpu.VMEM((slot_rows, feat_dim), bf16),
            pltpu.VMEM((2 * layers, slot_rows, feat_dim), f32),
            pltpu.VMEM((2 * layers, slot_rows, feat_dim), f32),
            pltpu.VMEM(block, bf16),
            pltpu.VMEM(block, bf16),
            pltpu.VMEM(block, bf16),
            pltpu.VMEM((2,) + square, f32),
            pltpu.VMEM(square, bf16),
            pltpu.VMEM(square, bf16),
            pltpu.VMEM(square, bf16),
            pltpu.VMEM(square, bf16),
            pltpu.VMEM((2,) + square, bf16),
            dma((layers,)), dma((layers,)), dma((layers,)), dma((layers,)),
            dma((2 * layers,)), dma((2 * layers,)),
            dma((5, layers)), dma((5, layers)),
            dma, dma, dma, dma,
            dma, dma((chips,)), dma, dma((chips,)),
        ],
        compiler_params=pltpu.CompilerParams(
            collective_id=0, has_side_effects=True, vmem_limit_bytes=56 * 1024 * 1024
        ),
        cost_estimate=pl.CostEstimate(flops=6 * 10**9, bytes_accessed=10**7, transcendentals=10**6),
    )(
        features, w_self[0], w_neigh[0], w_out,
        pick(labels, me)[:, None], pick(train_mask, me)[:, None],
        adjacency, adjacency.T, selector, selector.T,
    )
    return out[0][None], out[1][None], out[2][None], out[3][None]


def solution(mesh):
    in_specs = (
        P(None, "node", None),
        P("layer", None, None),
        P("layer", None, None),
        P(),
        P(None, "node"),
        P(None, "node"),
        P(None, "node", None, None),
        P(None, "node", None, None, None, None),
        P(None, "node", None, None),
        P(None, "node", None),
    )
    out_specs = (
        P("layer", None, "node", None),
        P("layer", None, "node", None),
        P("layer", None, None),
        P("layer", None, None),
    )
    return jax.shard_map(body, mesh=mesh, in_specs=in_specs, out_specs=out_specs, check_vma=False)
```

```python
import functools

import jax
import jax.numpy as jnp
from jax import lax
from jax.experimental import pallas as pl
from jax.experimental.pallas import tpu as pltpu
from jax.sharding import PartitionSpec as P


def dot(a, b, dims=((1,), (0,))):
    return lax.dot_general(a, b, (dims, ((), ())), preferred_element_type=jnp.float32)


MESH = pl.DeviceIdType.MESH


def window_kernel(
    layers, peers, slots, classes,
    feats, w_self, w_neigh, w_out, labels, mask, cols, vals, rows,
    acts_out, grads_out, final,
    adj, adj_t, sel, sel_t,
    hid, agg, pre, dpre, dout, wts, ext, back, outbox, inbox, rec_hid, rec_agg, rec_dpre,
    gsum, gsend, gsib, chip, parts,
    w_send, w_recv, f_send, f_recv, x_send, x_recv, blk_send, blk_recv,
    sib_send, sib_recv, rs_send, rs_recv, ag_send, ag_recv, fw_send, fw_recv,
):
    me = lax.axis_index("layer")
    node = lax.axis_index("node")
    core = lax.rem(node, 2)
    chip_at = node // 2
    chips = peers // 2
    sibling = node + 1 - 2 * core
    node_rows, feat_dim = hid.shape[1:]
    f32, bf16 = jnp.float32, jnp.bfloat16
    chunk = feat_dim // chips

    def remote(src, dst, send, recv, device):
        return pltpu.make_async_remote_copy(
            src_ref=src, dst_ref=dst, send_sem=send, recv_sem=recv, device_id=device, device_id_type=MESH
        )

    def drain(ref, sem):
        pltpu.make_async_copy(ref, ref, sem).wait()

    def each(count, fn, start=0):
        def step(i, carry):
            fn(i)
            return carry
        lax.fori_loop(start, count, step, 0)

    def other_layers(fn):
        each(layers, lambda i: fn(lax.rem(me + i, layers)), 1)

    def other_nodes(fn):
        each(peers, lambda i: fn(lax.rem(node + i, peers)), 1)

    def other_chips(fn):
        each(chips, lambda i: fn(lax.rem(chip_at + i, chips)), 1)

    barrier = pltpu.get_barrier_semaphore()
    other_layers(lambda i: pl.semaphore_signal(barrier, inc=1, device_id=(i, node), device_id_type=MESH))
    other_nodes(lambda i: pl.semaphore_signal(barrier, inc=1, device_id=(me, i), device_id_type=MESH))
    wts[me, 0] = w_self[0]
    wts[me, 1] = w_neigh[0]
    pl.semaphore_wait(barrier, layers - 1 + peers - 1)

    def send_weights(i):
        remote(wts.at[me, core], wts.at[me, core], w_send.at[i], w_recv.at[me], (i, node)).start()

    other_layers(send_weights)

    hid[0] = feats[me]
    ext[...] = jnp.zeros_like(ext)
    back[...] = jnp.zeros_like(back)
    _, _, row_tiles, degree, tile, _ = vals.shape
    for r in range(row_tiles):
        for c in range(adj.shape[1] // tile):
            block = jnp.zeros((tile, tile), f32)
            for j in range(degree):
                block = block + vals[me, 0, r, j].astype(f32) * jnp.where(cols[me, 0, r, j] == c, 1.0, 0.0)
            adj[r * tile : (r + 1) * tile, c * tile : (c + 1) * tile] = block.astype(bf16)
            adj_t[c * tile : (c + 1) * tile, r * tile : (r + 1) * tile] = jnp.transpose(block).astype(bf16)
    hits = lax.broadcasted_iota(jnp.int32, sel_t.shape, 0) == rows[pl.ds(me, 1), :]
    hits = jnp.where(hits, 1.0, 0.0)
    sel_t[...] = hits.astype(bf16)
    sel[...] = jnp.transpose(hits).astype(bf16)

    @pl.when(me == 0)
    def _():
        rec_hid[...] = feats[...]

    def swap_start(turn):
        def send(i):
            remote(
                outbox.at[turn, pl.ds(pl.multiple_of(i * slots, slots), slots)],
                inbox.at[turn, pl.ds(pl.multiple_of(node * slots, slots), slots)],
                x_send.at[turn], x_recv.at[turn], (me, i),
            ).start()
        other_nodes(send)
        mine = pl.ds(pl.multiple_of(node * slots, slots), slots)
        inbox[turn, mine] = outbox[turn, mine]

    def swap_bytes(turn):
        return inbox.at[turn, pl.ds(0, (peers - 1) * slots)]

    def give(kind, src, dst, owner):
        @pl.when(owner == me)
        def _():
            dst[me] = src[...]

        @pl.when(owner != me)
        def _():
            remote(src, dst.at[me], blk_send.at[kind, owner], blk_recv.at[kind, me], (owner, node)).start()

    def forward(layer):
        outbox[layer] = dot(sel[...], hid[layer])
        swap_start(layer)

        @pl.when(layer != me)
        def _():
            drain(wts.at[layer, core], w_recv.at[layer])
            remote(wts.at[layer, core], wts.at[layer, core], f_send.at[layer], f_recv.at[layer], (me, sibling)).start()

        ext[:node_rows] = hid[layer]
        drain(swap_bytes(layer), x_recv.at[layer])
        ext[node_rows : node_rows + peers * slots] = inbox[layer, : peers * slots].astype(bf16)
        aggregate = dot(adj[...], ext[...]).astype(bf16)
        agg[layer] = aggregate
        give(0, agg.at[layer], rec_agg, layer)

        @pl.when(layer != me)
        def _():
            drain(wts.at[layer, 1 - core], f_recv.at[layer])

        preact = dot(hid[layer], wts[layer, 0]) + dot(aggregate, wts[layer, 1])
        pre[layer] = preact
        hid[layer + 1] = (preact * jax.nn.sigmoid(preact)).astype(bf16)
        give(1, hid.at[layer + 1], acts_out, layer)

        @pl.when(layer + 1 < layers)
        def _():
            give(2, hid.at[layer + 1], rec_hid, lax.rem(layer + 1, layers))

    each(layers, forward)

    logits = dot(hid[layers], w_out[...])
    real = lax.broadcasted_iota(jnp.int32, logits.shape, 1)
    expo = jnp.where(real < classes, jnp.exp(logits), 0.0)
    probs = expo / jnp.sum(expo, axis=-1, keepdims=True)
    wide = (logits.shape[1], node_rows)
    onehot = jnp.transpose(
        jnp.where(lax.broadcasted_iota(jnp.int32, wide, 0) == labels[pl.ds(me, 1), :], 1.0, 0.0)
    )
    trained = jnp.transpose(jnp.broadcast_to(mask[pl.ds(me, 1), :].astype(f32), wide))
    g_logits = (trained * (probs - onehot)).astype(bf16)
    dout[layers] = dot(g_logits, w_out[...], ((1,), (1,))).astype(bf16)

    def backward(turn):
        layer = layers - 1 - turn
        preact = pre[layer]
        sigma = jax.nn.sigmoid(preact)
        d_pre = (dout[layer + 1].astype(f32) * (sigma * (1.0 + preact * (1.0 - sigma)))).astype(bf16)
        dpre[layer] = d_pre
        d_agg = dot(d_pre, wts[layer, 1], ((1,), (1,))).astype(bf16)
        d_ext = dot(adj_t[...], d_agg)
        outbox[layers + turn] = d_ext[node_rows:]
        swap_start(layers + turn)
        give(3, dpre.at[layer], rec_dpre, layer)
        local = dot(d_pre, wts[layer, 0], ((1,), (1,))) + d_ext[:node_rows]
        drain(swap_bytes(layers + turn), x_recv.at[layers + turn])
        back[: peers * slots] = inbox[layers + turn, : peers * slots].astype(bf16)
        dout[layer] = (local + dot(sel_t[...], back[...])).astype(bf16)
        give(4, dout.at[layer], grads_out, layer)

    each(layers, backward)

    gsum[...] = jnp.zeros_like(gsum)

    def add_span(i):
        span = lax.rem(me + i, layers)

        @pl.when(i != 0)
        def _():
            drain(rec_agg.at[span], blk_recv.at[0, span])
            drain(rec_dpre.at[span], blk_recv.at[3, span])

            @pl.when(me != 0)
            def _():
                drain(rec_hid.at[span], blk_recv.at[2, span])

        over_rows = ((0,), (0,))
        gsum[0] += dot(rec_hid[span], rec_dpre[span], over_rows)
        gsum[1] += dot(rec_agg[span], rec_dpre[span], over_rows)

    each(layers, add_span)

    gsend[...] = gsum[1 - core].astype(bf16)
    to_sibling = remote(gsend, gsib, sib_send, sib_recv, (me, sibling))
    to_sibling.start()
    drain(gsib, sib_recv)
    chip[...] = (gsum[core] + gsib[...].astype(f32)).astype(bf16)

    def rows_of(i):
        return pl.ds(pl.multiple_of(i * chunk, chunk), chunk)

    def send_part(i):
        remote(chip.at[rows_of(i)], parts.at[rows_of(chip_at)], rs_send, rs_recv, (me, 2 * i + core)).start()

    other_chips(send_part)
    parts[rows_of(chip_at)] = chip[rows_of(chip_at)]
    drain(parts.at[pl.ds(0, (chips - 1) * chunk)], rs_recv)
    total = parts[pl.ds(0, chunk)].astype(f32)
    for i in range(1, chips):
        total = total + parts[pl.ds(i * chunk, chunk)].astype(f32)
    final[core, rows_of(chip_at)] = total.astype(bf16)

    def send_final(i):
        mine = final.at[core, rows_of(chip_at)]
        remote(mine, mine, ag_send, ag_recv.at[chip_at], (me, 2 * i + core)).start()

    def pass_on(i):
        piece = final.at[core, rows_of(i)]
        remote(piece, piece, fw_send, fw_recv.at[i], (me, sibling)).start()

    other_chips(send_final)
    pass_on(chip_at)

    def take_final(i):
        drain(final.at[core, rows_of(i)], ag_recv.at[i])
        pass_on(i)

    other_chips(take_final)
    each(chips, lambda i: drain(final.at[1 - core, rows_of(i)], fw_recv.at[i]))

    def finish_layer(i):
        drain(acts_out.at[i], blk_recv.at[1, i])
        drain(grads_out.at[i], blk_recv.at[4, i])
        drain(wts.at[me, core], w_send.at[i])
        drain(wts.at[i, core], f_send.at[i])
        drain(agg.at[i], blk_send.at[0, i])
        drain(hid.at[i], blk_send.at[1, i])
        drain(dpre.at[i], blk_send.at[3, i])
        drain(dout.at[i], blk_send.at[4, i])

        @pl.when(i != 0)
        def _():
            drain(hid.at[i], blk_send.at[2, i])

    other_layers(finish_layer)
    each(2 * layers, lambda turn: drain(swap_bytes(turn), x_send.at[turn]))
    drain(gsend, sib_send)
    drain(parts.at[pl.ds(0, (chips - 1) * chunk)], rs_send)
    drain(final.at[0, pl.ds(0, (chips - 1) * chunk)], ag_send)
    drain(final.at[0], fw_send)


def body(features, w_self, w_neigh, w_out, labels, train_mask, tile_cols, tile_vals, send_rows, send_counts):
    layers = lax.axis_size("layer")
    peers = lax.axis_size("node")
    spans, node_rows, feat_dim = features.shape
    classes = w_out.shape[1]
    tile = tile_vals.shape[-1]
    slots = send_rows.shape[-1]
    ext_rows = (node_rows + peers * slots + tile - 1) // tile * tile
    slot_rows = ext_rows - node_rows
    chips = peers // 2
    chunk = feat_dim // chips
    scale = 1.0 / (spans * node_rows * peers)
    f32, bf16 = jnp.float32, jnp.bfloat16

    live = jnp.arange(slots) < send_counts[:, 0, :, None]
    slot_of = jnp.where(live, send_rows[:, 0], -1).reshape(spans, peers * slots)
    slot_of = jnp.pad(slot_of, ((0, 0), (0, slot_rows - peers * slots)), constant_values=-1)
    w_out = jnp.pad(w_out, ((0, 0), (0, -classes % 128)))
    block = (layers, node_rows, feat_dim)
    square = (feat_dim, feat_dim)
    vmem = pl.BlockSpec(memory_space=pltpu.VMEM)
    dma = pltpu.SemaphoreType.DMA
    out = pl.pallas_call(
        functools.partial(window_kernel, layers, peers, slots, classes),
        out_shape=(
            jax.ShapeDtypeStruct(block, bf16),
            jax.ShapeDtypeStruct(block, bf16),
            jax.ShapeDtypeStruct((2,) + square, bf16),
        ),
        in_specs=[vmem] * 6 + [pl.BlockSpec(memory_space=pltpu.SMEM)] + [vmem] * 2,
        out_specs=[vmem] * 3,
        scratch_shapes=[
            pltpu.VMEM((node_rows, ext_rows), bf16),
            pltpu.VMEM((ext_rows, node_rows), bf16),
            pltpu.VMEM((slot_rows, node_rows), bf16),
            pltpu.VMEM((node_rows, slot_rows), bf16),
            pltpu.VMEM((layers + 1, node_rows, feat_dim), bf16),
            pltpu.VMEM(block, bf16),
            pltpu.VMEM(block, f32),
            pltpu.VMEM(block, bf16),
            pltpu.VMEM((layers + 1, node_rows, feat_dim), bf16),
            pltpu.VMEM((layers, 2) + square, bf16),
            pltpu.VMEM((ext_rows, feat_dim), bf16),
            pltpu.VMEM((slot_rows, feat_dim), bf16),
            pltpu.VMEM((2 * layers, slot_rows, feat_dim), f32),
            pltpu.VMEM((2 * layers, slot_rows, feat_dim), f32),
            pltpu.VMEM(block, bf16),
            pltpu.VMEM(block, bf16),
            pltpu.VMEM(block, bf16),
            pltpu.VMEM((2,) + square, f32),
            pltpu.VMEM(square, bf16),
            pltpu.VMEM(square, bf16),
            pltpu.VMEM(square, bf16),
            pltpu.VMEM(square, bf16),
            dma((layers,)), dma((layers,)), dma((layers,)), dma((layers,)),
            dma((2 * layers,)), dma((2 * layers,)),
            dma((5, layers)), dma((5, layers)),
            dma, dma, dma, dma,
            dma, dma((chips,)), dma, dma((chips,)),
        ],
        compiler_params=pltpu.CompilerParams(
            collective_id=0, has_side_effects=True, vmem_limit_bytes=56 * 1024 * 1024
        ),
        cost_estimate=pl.CostEstimate(flops=6 * 10**9, bytes_accessed=10**7, transcendentals=10**6),
    )(
        features, w_self, w_neigh, w_out, labels, train_mask, tile_cols, tile_vals, slot_of,
    )
    return out[0][None], out[1][None], out[2][:1].astype(f32) * scale, out[2][1:].astype(f32) * scale


def solution(mesh):
    in_specs = (
        P(None, "node", None),
        P("layer", None, None),
        P("layer", None, None),
        P(),
        P(None, "node"),
        P(None, "node"),
        P(None, "node", None, None),
        P(None, "node", None, None, None, None),
        P(None, "node", None, None),
        P(None, "node", None),
    )
    out_specs = (
        P("layer", None, "node", None),
        P("layer", None, "node", None),
        P("layer", None, None),
        P("layer", None, None),
    )
    return jax.shard_map(body, mesh=mesh, in_specs=in_specs, out_specs=out_specs, check_vma=False)
```

```python
import functools

import jax
import jax.numpy as jnp
from jax import lax
from jax.experimental import pallas as pl
from jax.experimental.pallas import tpu as pltpu
from jax.sharding import PartitionSpec as P


def dot(a, b, dims=((1,), (0,))):
    return lax.dot_general(a, b, (dims, ((), ())), preferred_element_type=jnp.float32)


MESH = pl.DeviceIdType.MESH


def window_kernel(
    layers, peers, slots, classes,
    feats, w_self, w_neigh, w_out, labels, mask, cols, vals, rows,
    acts_out, grads_out, final,
    adj, adj_t, sel, sel_t,
    hid, agg, pre, dpre, dout, wts, ext, back, outbox, inbox, rec, rec_dpre,
    gsum, gsend, gsib, chip, parts,
    w_send, w_recv, f_send, f_recv, x_send, x_recv, blk_send, blk_recv,
    sib_send, sib_recv, rs_send, rs_recv, ag_send, ag_recv, fw_send, fw_recv,
):
    me = lax.axis_index("layer")
    node = lax.axis_index("node")
    core = lax.rem(node, 2)
    chip_at = node // 2
    chips = peers // 2
    sibling = node + 1 - 2 * core
    node_rows, feat_dim = hid.shape[1:]
    f32, bf16 = jnp.float32, jnp.bfloat16
    chunk = feat_dim // chips

    def remote(src, dst, send, recv, device):
        return pltpu.make_async_remote_copy(
            src_ref=src, dst_ref=dst, send_sem=send, recv_sem=recv, device_id=device, device_id_type=MESH
        )

    def drain(ref, sem):
        pltpu.make_async_copy(ref, ref, sem).wait()

    def each(count, fn, start=0):
        def step(i, carry):
            fn(i)
            return carry
        lax.fori_loop(start, count, step, 0)

    def other_layers(fn):
        each(layers, lambda i: fn(lax.rem(me + i, layers)), 1)

    def other_nodes(fn):
        each(peers, lambda i: fn(lax.rem(node + i, peers)), 1)

    def other_chips(fn):
        each(chips, lambda i: fn(lax.rem(chip_at + i, chips)), 1)

    barrier = pltpu.get_barrier_semaphore()
    other_layers(lambda i: pl.semaphore_signal(barrier, inc=1, device_id=(i, node), device_id_type=MESH))
    other_nodes(lambda i: pl.semaphore_signal(barrier, inc=1, device_id=(me, i), device_id_type=MESH))
    wts[me, 0] = w_self[0]
    wts[me, 1] = w_neigh[0]
    pl.semaphore_wait(barrier, layers - 1 + peers - 1)

    def send_weights(i):
        remote(wts.at[me, core], wts.at[me, core], w_send.at[i], w_recv.at[me], (i, node)).start()

    other_layers(send_weights)

    hid[0] = feats[me]
    ext[...] = jnp.zeros_like(ext)
    back[...] = jnp.zeros_like(back)
    _, _, row_tiles, degree, tile, _ = vals.shape
    for r in range(row_tiles):
        for c in range(adj.shape[1] // tile):
            block = jnp.zeros((tile, tile), f32)
            for j in range(degree):
                block = block + vals[me, 0, r, j].astype(f32) * jnp.where(cols[me, 0, r, j] == c, 1.0, 0.0)
            adj[r * tile : (r + 1) * tile, c * tile : (c + 1) * tile] = block.astype(bf16)
            adj_t[c * tile : (c + 1) * tile, r * tile : (r + 1) * tile] = jnp.transpose(block).astype(bf16)
    hits = lax.broadcasted_iota(jnp.int32, sel_t.shape, 0) == rows[pl.ds(me, 1), :]
    hits = jnp.where(hits, 1.0, 0.0)
    sel_t[...] = hits.astype(bf16)
    sel[...] = jnp.transpose(hits).astype(bf16)

    @pl.when(me == 0)
    def _():
        rec[0] = feats[...]

    def swap_start(turn):
        def send(i):
            remote(
                outbox.at[turn, pl.ds(pl.multiple_of(i * slots, slots), slots)],
                inbox.at[turn, pl.ds(pl.multiple_of(node * slots, slots), slots)],
                x_send.at[turn], x_recv.at[turn], (me, i),
            ).start()
        other_nodes(send)
        mine = pl.ds(pl.multiple_of(node * slots, slots), slots)
        inbox[turn, mine] = outbox[turn, mine]

    def swap_bytes(turn):
        return inbox.at[turn, pl.ds(0, (peers - 1) * slots)]

    def give(kind, src, dst, owner):
        @pl.when(owner == me)
        def _():
            dst[me] = src[...]

        @pl.when(owner != me)
        def _():
            remote(src, dst.at[me], blk_send.at[kind, owner], blk_recv.at[kind, me], (owner, node)).start()

    def forward(layer):
        outbox[layer] = dot(sel[...], hid[layer])
        swap_start(layer)

        @pl.when(layer != me)
        def _():
            drain(wts.at[layer, core], w_recv.at[layer])
            remote(wts.at[layer, core], wts.at[layer, core], f_send.at[layer], f_recv.at[layer], (me, sibling)).start()

        ext[:node_rows] = hid[layer]
        drain(swap_bytes(layer), x_recv.at[layer])
        ext[node_rows : node_rows + peers * slots] = inbox[layer, : peers * slots].astype(bf16)
        aggregate = dot(adj[...], ext[...]).astype(bf16)
        agg[layer] = aggregate
        give(0, agg.at[layer], rec.at[1], layer)

        @pl.when(layer != me)
        def _():
            drain(wts.at[layer, 1 - core], f_recv.at[layer])

        preact = dot(hid[layer], wts[layer, 0]) + dot(aggregate, wts[layer, 1])
        pre[layer] = preact
        hid[layer + 1] = (preact * jax.nn.sigmoid(preact)).astype(bf16)
        give(1, hid.at[layer + 1], acts_out, layer)

        @pl.when(layer + 1 < layers)
        def _():
            give(2, hid.at[layer + 1], rec.at[0], lax.rem(layer + 1, layers))

    each(layers, forward)

    logits = dot(hid[layers], w_out[...])
    real = lax.broadcasted_iota(jnp.int32, logits.shape, 1)
    expo = jnp.where(real < classes, jnp.exp(logits), 0.0)
    probs = expo / jnp.sum(expo, axis=-1, keepdims=True)
    wide = (logits.shape[1], node_rows)
    onehot = jnp.transpose(
        jnp.where(lax.broadcasted_iota(jnp.int32, wide, 0) == labels[pl.ds(me, 1), :], 1.0, 0.0)
    )
    trained = jnp.transpose(jnp.broadcast_to(mask[pl.ds(me, 1), :].astype(f32), wide))
    g_logits = (trained * (probs - onehot)).astype(bf16)
    dout[layers] = dot(g_logits, w_out[...], ((1,), (1,))).astype(bf16)

    def backward(turn):
        layer = layers - 1 - turn
        preact = pre[layer]
        sigma = jax.nn.sigmoid(preact)
        d_pre = (dout[layer + 1].astype(f32) * (sigma * (1.0 + preact * (1.0 - sigma)))).astype(bf16)
        dpre[layer] = d_pre
        d_agg = dot(d_pre, wts[layer, 1], ((1,), (1,))).astype(bf16)
        d_ext = dot(adj_t[...], d_agg)
        outbox[layers + turn] = d_ext[node_rows:]
        swap_start(layers + turn)
        give(3, dpre.at[layer], rec_dpre, layer)
        local = dot(d_pre, wts[layer, 0], ((1,), (1,))) + d_ext[:node_rows]
        drain(swap_bytes(layers + turn), x_recv.at[layers + turn])
        back[: peers * slots] = inbox[layers + turn, : peers * slots].astype(bf16)
        dout[layer] = (local + dot(sel_t[...], back[...])).astype(bf16)
        give(4, dout.at[layer], grads_out, layer)

    each(layers, backward)

    def take_span(span):
        drain(rec.at[1, span], blk_recv.at[0, span])
        drain(rec_dpre.at[span], blk_recv.at[3, span])

        @pl.when(me != 0)
        def _():
            drain(rec.at[0, span], blk_recv.at[2, span])

    other_layers(take_span)

    def weight_grad(side):
        left = rec[side].reshape(layers * node_rows, feat_dim)
        return dot(left, rec_dpre[...].reshape(layers * node_rows, feat_dim), ((0,), (0,)))

    gsend[...] = weight_grad(1 - core).astype(bf16)
    to_sibling = remote(gsend, gsib, sib_send, sib_recv, (me, sibling))
    to_sibling.start()
    gsum[...] = weight_grad(core)
    drain(gsib, sib_recv)
    chip[...] = (gsum[...] + gsib[...].astype(f32)).astype(bf16)

    def rows_of(i):
        return pl.ds(pl.multiple_of(i * chunk, chunk), chunk)

    def send_part(i):
        remote(chip.at[rows_of(i)], parts.at[rows_of(chip_at)], rs_send, rs_recv, (me, 2 * i + core)).start()

    other_chips(send_part)
    parts[rows_of(chip_at)] = chip[rows_of(chip_at)]
    drain(parts.at[pl.ds(0, (chips - 1) * chunk)], rs_recv)
    total = parts[pl.ds(0, chunk)].astype(f32)
    for i in range(1, chips):
        total = total + parts[pl.ds(i * chunk, chunk)].astype(f32)
    final[core, rows_of(chip_at)] = total.astype(bf16)

    def send_final(i):
        mine = final.at[core, rows_of(chip_at)]
        remote(mine, mine, ag_send, ag_recv.at[chip_at], (me, 2 * i + core)).start()

    def pass_on(i):
        piece = final.at[core, rows_of(i)]
        remote(piece, piece, fw_send, fw_recv.at[i], (me, sibling)).start()

    other_chips(send_final)
    pass_on(chip_at)

    def take_final(i):
        drain(final.at[core, rows_of(i)], ag_recv.at[i])
        pass_on(i)

    other_chips(take_final)
    each(chips, lambda i: drain(final.at[1 - core, rows_of(i)], fw_recv.at[i]))

    def finish_layer(i):
        drain(acts_out.at[i], blk_recv.at[1, i])
        drain(grads_out.at[i], blk_recv.at[4, i])
        drain(wts.at[me, core], w_send.at[i])
        drain(wts.at[i, core], f_send.at[i])
        drain(agg.at[i], blk_send.at[0, i])
        drain(hid.at[i], blk_send.at[1, i])
        drain(dpre.at[i], blk_send.at[3, i])
        drain(dout.at[i], blk_send.at[4, i])

        @pl.when(i != 0)
        def _():
            drain(hid.at[i], blk_send.at[2, i])

    other_layers(finish_layer)
    each(2 * layers, lambda turn: drain(swap_bytes(turn), x_send.at[turn]))
    drain(gsend, sib_send)
    drain(parts.at[pl.ds(0, (chips - 1) * chunk)], rs_send)
    drain(final.at[0, pl.ds(0, (chips - 1) * chunk)], ag_send)
    drain(final.at[0], fw_send)


def body(features, w_self, w_neigh, w_out, labels, train_mask, tile_cols, tile_vals, send_rows, send_counts):
    layers = lax.axis_size("layer")
    peers = lax.axis_size("node")
    spans, node_rows, feat_dim = features.shape
    classes = w_out.shape[1]
    tile = tile_vals.shape[-1]
    slots = send_rows.shape[-1]
    ext_rows = (node_rows + peers * slots + tile - 1) // tile * tile
    slot_rows = ext_rows - node_rows
    chips = peers // 2
    chunk = feat_dim // chips
    scale = 1.0 / (spans * node_rows * peers)
    f32, bf16 = jnp.float32, jnp.bfloat16

    live = jnp.arange(slots) < send_counts[:, 0, :, None]
    slot_of = jnp.where(live, send_rows[:, 0], -1).reshape(spans, peers * slots)
    slot_of = jnp.pad(slot_of, ((0, 0), (0, slot_rows - peers * slots)), constant_values=-1)
    w_out = jnp.pad(w_out, ((0, 0), (0, -classes % 128)))
    block = (layers, node_rows, feat_dim)
    square = (feat_dim, feat_dim)
    vmem = pl.BlockSpec(memory_space=pltpu.VMEM)
    dma = pltpu.SemaphoreType.DMA
    out = pl.pallas_call(
        functools.partial(window_kernel, layers, peers, slots, classes),
        out_shape=(
            jax.ShapeDtypeStruct(block, bf16),
            jax.ShapeDtypeStruct(block, bf16),
            jax.ShapeDtypeStruct((2,) + square, bf16),
        ),
        in_specs=[vmem] * 6 + [pl.BlockSpec(memory_space=pltpu.SMEM)] + [vmem] * 2,
        out_specs=[vmem] * 3,
        scratch_shapes=[
            pltpu.VMEM((node_rows, ext_rows), bf16),
            pltpu.VMEM((ext_rows, node_rows), bf16),
            pltpu.VMEM((slot_rows, node_rows), bf16),
            pltpu.VMEM((node_rows, slot_rows), bf16),
            pltpu.VMEM((layers + 1, node_rows, feat_dim), bf16),
            pltpu.VMEM(block, bf16),
            pltpu.VMEM(block, f32),
            pltpu.VMEM(block, bf16),
            pltpu.VMEM((layers + 1, node_rows, feat_dim), bf16),
            pltpu.VMEM((layers, 2) + square, bf16),
            pltpu.VMEM((ext_rows, feat_dim), bf16),
            pltpu.VMEM((slot_rows, feat_dim), bf16),
            pltpu.VMEM((2 * layers, slot_rows, feat_dim), f32),
            pltpu.VMEM((2 * layers, slot_rows, feat_dim), f32),
            pltpu.VMEM((2,) + block, bf16),
            pltpu.VMEM(block, bf16),
            pltpu.VMEM(square, f32),
            pltpu.VMEM(square, bf16),
            pltpu.VMEM(square, bf16),
            pltpu.VMEM(square, bf16),
            pltpu.VMEM(square, bf16),
            dma((layers,)), dma((layers,)), dma((layers,)), dma((layers,)),
            dma((2 * layers,)), dma((2 * layers,)),
            dma((5, layers)), dma((5, layers)),
            dma, dma, dma, dma,
            dma, dma((chips,)), dma, dma((chips,)),
        ],
        compiler_params=pltpu.CompilerParams(
            collective_id=0, has_side_effects=True, vmem_limit_bytes=56 * 1024 * 1024
        ),
        cost_estimate=pl.CostEstimate(flops=6 * 10**9, bytes_accessed=10**7, transcendentals=10**6),
    )(
        features, w_self, w_neigh, w_out, labels, train_mask, tile_cols, tile_vals, slot_of,
    )
    return out[0][None], out[1][None], out[2][:1].astype(f32) * scale, out[2][1:].astype(f32) * scale


def solution(mesh):
    in_specs = (
        P(None, "node", None),
        P("layer", None, None),
        P("layer", None, None),
        P(),
        P(None, "node"),
        P(None, "node"),
        P(None, "node", None, None),
        P(None, "node", None, None, None, None),
        P(None, "node", None, None),
        P(None, "node", None),
    )
    out_specs = (
        P("layer", None, "node", None),
        P("layer", None, "node", None),
        P("layer", None, None),
        P("layer", None, None),
    )
    return jax.shard_map(body, mesh=mesh, in_specs=in_specs, out_specs=out_specs, check_vma=False)
```

```python
import functools

import jax
import jax.numpy as jnp
from jax import lax
from jax.experimental import pallas as pl
from jax.experimental.pallas import tpu as pltpu
from jax.sharding import PartitionSpec as P


def dot(a, b, dims=((1,), (0,))):
    return lax.dot_general(a, b, (dims, ((), ())), preferred_element_type=jnp.float32)


MESH = pl.DeviceIdType.MESH


def window_kernel(
    layers, peers, slots, classes,
    feats, w_self, w_neigh, w_out, labels, mask, cols, vals, rows,
    acts_out, grads_out, final,
    adj, adj_t, sel, sel_t,
    hid, agg, pre, dpre, dout, wts, ext, back, outbox, inbox, rec_hid, rec_agg, rec_dpre,
    gsum, gsend, gsib, chip, parts,
    w_send, w_recv, f_send, f_recv, x_send, x_recv, blk_send, blk_recv,
    sib_send, sib_recv, rs_send, rs_recv, ag_send, ag_recv, fw_send, fw_recv,
):
    me = lax.axis_index("layer")
    node = lax.axis_index("node")
    core = lax.rem(node, 2)
    chip_at = node // 2
    chips = peers // 2
    sibling = node + 1 - 2 * core
    node_rows, feat_dim = hid.shape[1:]
    f32, bf16 = jnp.float32, jnp.bfloat16
    chunk = feat_dim // chips

    def remote(src, dst, send, recv, device):
        return pltpu.make_async_remote_copy(
            src_ref=src, dst_ref=dst, send_sem=send, recv_sem=recv, device_id=device, device_id_type=MESH
        )

    def drain(ref, sem):
        pltpu.make_async_copy(ref, ref, sem).wait()

    def each(count, fn, start=0):
        def step(i, carry):
            fn(i)
            return carry
        lax.fori_loop(start, count, step, 0)

    def other_layers(fn):
        each(layers, lambda i: fn(lax.rem(me + i, layers)), 1)

    def other_nodes(fn):
        each(peers, lambda i: fn(lax.rem(node + i, peers)), 1)

    def other_chips(fn):
        each(chips, lambda i: fn(lax.rem(chip_at + i, chips)), 1)

    barrier = pltpu.get_barrier_semaphore()
    other_layers(lambda i: pl.semaphore_signal(barrier, inc=1, device_id=(i, node), device_id_type=MESH))
    other_nodes(lambda i: pl.semaphore_signal(barrier, inc=1, device_id=(me, i), device_id_type=MESH))
    wts[me, 0] = w_self[0]
    wts[me, 1] = w_neigh[0]
    pl.semaphore_wait(barrier, layers - 1 + peers - 1)

    def send_weights(i):
        remote(wts.at[me, core], wts.at[me, core], w_send.at[i], w_recv.at[me], (i, node)).start()

    other_layers(send_weights)

    hid[0] = feats[me]
    ext[...] = jnp.zeros_like(ext)
    back[...] = jnp.zeros_like(back)
    _, _, row_tiles, degree, tile, _ = vals.shape
    for r in range(row_tiles):
        for c in range(adj.shape[1] // tile):
            block = jnp.zeros((tile, tile), f32)
            for j in range(degree):
                block = block + vals[me, 0, r, j].astype(f32) * jnp.where(cols[me, 0, r, j] == c, 1.0, 0.0)
            adj[r * tile : (r + 1) * tile, c * tile : (c + 1) * tile] = block.astype(bf16)
            adj_t[c * tile : (c + 1) * tile, r * tile : (r + 1) * tile] = jnp.transpose(block).astype(bf16)
    hits = lax.broadcasted_iota(jnp.int32, sel_t.shape, 0) == rows[pl.ds(me, 1), :]
    hits = jnp.where(hits, 1.0, 0.0)
    sel_t[...] = hits.astype(bf16)
    sel[...] = jnp.transpose(hits).astype(bf16)

    @pl.when(me == 0)
    def _():
        rec_hid[...] = feats[...]

    def swap_start(turn):
        def send(i):
            remote(
                outbox.at[turn, pl.ds(pl.multiple_of(i * slots, slots), slots)],
                inbox.at[turn, pl.ds(pl.multiple_of(node * slots, slots), slots)],
                x_send.at[turn], x_recv.at[turn], (me, i),
            ).start()
        other_nodes(send)
        mine = pl.ds(pl.multiple_of(node * slots, slots), slots)
        inbox[turn, mine] = outbox[turn, mine]

    def swap_bytes(turn):
        return inbox.at[turn, pl.ds(0, (peers - 1) * slots)]

    def give(kind, src, dst, owner):
        @pl.when(owner == me)
        def _():
            dst[me] = src[...]

        @pl.when(owner != me)
        def _():
            remote(src, dst.at[me], blk_send.at[kind, owner], blk_recv.at[kind, me], (owner, node)).start()

    def slope(preact):
        sigma = jax.nn.sigmoid(preact)
        return sigma * (1.0 + preact * (1.0 - sigma))

    def forward(layer):
        outbox[layer] = dot(sel[...], hid[layer])
        swap_start(layer)

        @pl.when(layer != me)
        def _():
            drain(wts.at[layer, core], w_recv.at[layer])
            remote(wts.at[layer, core], wts.at[layer, core], f_send.at[layer], f_recv.at[layer], (me, sibling)).start()

        ext[:node_rows] = hid[layer]

        @pl.when(layer > 0)
        def _():
            pre[layer - 1] = slope(pre[layer - 1])

        @pl.when(layer != me)
        def _():
            drain(wts.at[layer, 1 - core], f_recv.at[layer])

        pre[layer] = dot(hid[layer], wts[layer, 0])
        drain(swap_bytes(layer), x_recv.at[layer])
        ext[node_rows : node_rows + peers * slots] = inbox[layer, : peers * slots].astype(bf16)
        aggregate = dot(adj[...], ext[...]).astype(bf16)
        agg[layer] = aggregate
        give(0, agg.at[layer], rec_agg, layer)

        preact = pre[layer] + dot(aggregate, wts[layer, 1])
        pre[layer] = preact
        hid[layer + 1] = (preact * jax.nn.sigmoid(preact)).astype(bf16)
        give(1, hid.at[layer + 1], acts_out, layer)

        @pl.when(layer + 1 < layers)
        def _():
            give(2, hid.at[layer + 1], rec_hid, lax.rem(layer + 1, layers))

    each(layers, forward)
    pre[layers - 1] = slope(pre[layers - 1])

    logits = dot(hid[layers], w_out[...])
    real = lax.broadcasted_iota(jnp.int32, logits.shape, 1)
    expo = jnp.where(real < classes, jnp.exp(logits), 0.0)
    probs = expo / jnp.sum(expo, axis=-1, keepdims=True)
    wide = (logits.shape[1], node_rows)
    onehot = jnp.transpose(
        jnp.where(lax.broadcasted_iota(jnp.int32, wide, 0) == labels[pl.ds(me, 1), :], 1.0, 0.0)
    )
    trained = jnp.transpose(jnp.broadcast_to(mask[pl.ds(me, 1), :].astype(f32), wide))
    g_logits = (trained * (probs - onehot)).astype(bf16)
    dout[layers] = dot(g_logits, w_out[...], ((1,), (1,))).astype(bf16)

    def backward(turn):
        layer = layers - 1 - turn
        d_pre = (dout[layer + 1].astype(f32) * pre[layer]).astype(bf16)
        dpre[layer] = d_pre
        d_agg = dot(d_pre, wts[layer, 1], ((1,), (1,))).astype(bf16)
        d_ext = dot(adj_t[...], d_agg)
        outbox[layers + turn] = d_ext[node_rows:]
        swap_start(layers + turn)
        give(3, dpre.at[layer], rec_dpre, layer)
        local = dot(d_pre, wts[layer, 0], ((1,), (1,))) + d_ext[:node_rows]
        drain(swap_bytes(layers + turn), x_recv.at[layers + turn])
        back[: peers * slots] = inbox[layers + turn, : peers * slots].astype(bf16)
        dout[layer] = (local + dot(sel_t[...], back[...])).astype(bf16)
        give(4, dout.at[layer], grads_out, layer)

    each(layers, backward)

    gsum[...] = jnp.zeros_like(gsum)

    def add_span(i):
        span = lax.rem(me + i, layers)

        @pl.when(i != 0)
        def _():
            drain(rec_agg.at[span], blk_recv.at[0, span])
            drain(rec_dpre.at[span], blk_recv.at[3, span])

            @pl.when(me != 0)
            def _():
                drain(rec_hid.at[span], blk_recv.at[2, span])

        over_rows = ((0,), (0,))
        gsum[0] += dot(rec_hid[span], rec_dpre[span], over_rows)
        gsum[1] += dot(rec_agg[span], rec_dpre[span], over_rows)

    each(layers, add_span)

    gsend[...] = gsum[1 - core].astype(bf16)
    to_sibling = remote(gsend, gsib, sib_send, sib_recv, (me, sibling))
    to_sibling.start()
    drain(gsib, sib_recv)
    chip[...] = (gsum[core] + gsib[...].astype(f32)).astype(bf16)

    def rows_of(i):
        return pl.ds(pl.multiple_of(i * chunk, chunk), chunk)

    def send_part(i):
        remote(chip.at[rows_of(i)], parts.at[rows_of(chip_at)], rs_send, rs_recv, (me, 2 * i + core)).start()

    other_chips(send_part)
    parts[rows_of(chip_at)] = chip[rows_of(chip_at)]
    drain(parts.at[pl.ds(0, (chips - 1) * chunk)], rs_recv)
    total = parts[pl.ds(0, chunk)].astype(f32)
    for i in range(1, chips):
        total = total + parts[pl.ds(i * chunk, chunk)].astype(f32)
    final[core, rows_of(chip_at)] = total.astype(bf16)

    def send_final(i):
        mine = final.at[core, rows_of(chip_at)]
        remote(mine, mine, ag_send, ag_recv.at[chip_at], (me, 2 * i + core)).start()

    def pass_on(i):
        piece = final.at[core, rows_of(i)]
        remote(piece, piece, fw_send, fw_recv.at[i], (me, sibling)).start()

    other_chips(send_final)
    pass_on(chip_at)

    def take_final(i):
        drain(final.at[core, rows_of(i)], ag_recv.at[i])
        pass_on(i)

    other_chips(take_final)
    each(chips, lambda i: drain(final.at[1 - core, rows_of(i)], fw_recv.at[i]))

    def finish_layer(i):
        drain(acts_out.at[i], blk_recv.at[1, i])
        drain(grads_out.at[i], blk_recv.at[4, i])
        drain(wts.at[me, core], w_send.at[i])
        drain(wts.at[i, core], f_send.at[i])
        drain(agg.at[i], blk_send.at[0, i])
        drain(hid.at[i], blk_send.at[1, i])
        drain(dpre.at[i], blk_send.at[3, i])
        drain(dout.at[i], blk_send.at[4, i])

        @pl.when(i != 0)
        def _():
            drain(hid.at[i], blk_send.at[2, i])

    other_layers(finish_layer)
    each(2 * layers, lambda turn: drain(swap_bytes(turn), x_send.at[turn]))
    drain(gsend, sib_send)
    drain(parts.at[pl.ds(0, (chips - 1) * chunk)], rs_send)
    drain(final.at[0, pl.ds(0, (chips - 1) * chunk)], ag_send)
    drain(final.at[0], fw_send)


def body(features, w_self, w_neigh, w_out, labels, train_mask, tile_cols, tile_vals, send_rows, send_counts):
    layers = lax.axis_size("layer")
    peers = lax.axis_size("node")
    spans, node_rows, feat_dim = features.shape
    classes = w_out.shape[1]
    tile = tile_vals.shape[-1]
    slots = send_rows.shape[-1]
    ext_rows = (node_rows + peers * slots + tile - 1) // tile * tile
    slot_rows = ext_rows - node_rows
    chips = peers // 2
    chunk = feat_dim // chips
    scale = 1.0 / (spans * node_rows * peers)
    f32, bf16 = jnp.float32, jnp.bfloat16

    live = jnp.arange(slots) < send_counts[:, 0, :, None]
    slot_of = jnp.where(live, send_rows[:, 0], -1).reshape(spans, peers * slots)
    slot_of = jnp.pad(slot_of, ((0, 0), (0, slot_rows - peers * slots)), constant_values=-1)
    w_out = jnp.pad(w_out, ((0, 0), (0, -classes % 128)))
    block = (layers, node_rows, feat_dim)
    square = (feat_dim, feat_dim)
    vmem = pl.BlockSpec(memory_space=pltpu.VMEM)
    dma = pltpu.SemaphoreType.DMA
    out = pl.pallas_call(
        functools.partial(window_kernel, layers, peers, slots, classes),
        out_shape=(
            jax.ShapeDtypeStruct(block, bf16),
            jax.ShapeDtypeStruct(block, bf16),
            jax.ShapeDtypeStruct((2,) + square, bf16),
        ),
        in_specs=[vmem] * 6 + [pl.BlockSpec(memory_space=pltpu.SMEM)] + [vmem] * 2,
        out_specs=[vmem] * 3,
        scratch_shapes=[
            pltpu.VMEM((node_rows, ext_rows), bf16),
            pltpu.VMEM((ext_rows, node_rows), bf16),
            pltpu.VMEM((slot_rows, node_rows), bf16),
            pltpu.VMEM((node_rows, slot_rows), bf16),
            pltpu.VMEM((layers + 1, node_rows, feat_dim), bf16),
            pltpu.VMEM(block, bf16),
            pltpu.VMEM(block, f32),
            pltpu.VMEM(block, bf16),
            pltpu.VMEM((layers + 1, node_rows, feat_dim), bf16),
            pltpu.VMEM((layers, 2) + square, bf16),
            pltpu.VMEM((ext_rows, feat_dim), bf16),
            pltpu.VMEM((slot_rows, feat_dim), bf16),
            pltpu.VMEM((2 * layers, slot_rows, feat_dim), f32),
            pltpu.VMEM((2 * layers, slot_rows, feat_dim), f32),
            pltpu.VMEM(block, bf16),
            pltpu.VMEM(block, bf16),
            pltpu.VMEM(block, bf16),
            pltpu.VMEM((2,) + square, f32),
            pltpu.VMEM(square, bf16),
            pltpu.VMEM(square, bf16),
            pltpu.VMEM(square, bf16),
            pltpu.VMEM(square, bf16),
            dma((layers,)), dma((layers,)), dma((layers,)), dma((layers,)),
            dma((2 * layers,)), dma((2 * layers,)),
            dma((5, layers)), dma((5, layers)),
            dma, dma, dma, dma,
            dma, dma((chips,)), dma, dma((chips,)),
        ],
        compiler_params=pltpu.CompilerParams(
            collective_id=0, has_side_effects=True, vmem_limit_bytes=56 * 1024 * 1024
        ),
        cost_estimate=pl.CostEstimate(flops=6 * 10**9, bytes_accessed=10**7, transcendentals=10**6),
    )(
        features, w_self, w_neigh, w_out, labels, train_mask, tile_cols, tile_vals, slot_of,
    )
    return out[0][None], out[1][None], out[2][:1].astype(f32) * scale, out[2][1:].astype(f32) * scale


def solution(mesh):
    in_specs = (
        P(None, "node", None),
        P("layer", None, None),
        P("layer", None, None),
        P(),
        P(None, "node"),
        P(None, "node"),
        P(None, "node", None, None),
        P(None, "node", None, None, None, None),
        P(None, "node", None, None),
        P(None, "node", None),
    )
    out_specs = (
        P("layer", None, "node", None),
        P("layer", None, "node", None),
        P("layer", None, None),
        P("layer", None, None),
    )
    return jax.shard_map(body, mesh=mesh, in_specs=in_specs, out_specs=out_specs, check_vma=False)
```
